512 devices in a mesh: pts: 128 (over x_lo, z, y), dim: 4 (over x_hi, core).
Axes of the slice: x: 4 (x_hi: 2, x_lo: 2; x = x_hi * 2 + x_lo), y: 4, z: 16, core: 2. Of those that a mesh axis runs over, the one named last changes fastest.
Arguments:
- factors: bfloat16 [8, 262144, 256], P('dim', 'pts'), may hold values from -6 to 6
- tridiag: bfloat16 [8, 256, 256], P('dim'), may hold values from -0.5 to 1.5, as said below
- probe_vector: float32 [262144], P('pts'), may hold values from -0.03125 to 0.03125
- cotangent: float32 [4, 262144], P(None, 'pts'), may hold values from -1 to 1
Outputs:
- grad_factors: bfloat16 [8, 262144, 256], P('dim', 'pts')
The draws below stay inside these ranges and needn't reach their ends.
Inputs may be any that keep to these rules, and one draw needn't show every extreme that they name: `tridiag`: each T_d is symmetric tridiagonal with a dominant diagonal.
All inputs are finite; a program needn't handle non-finite values.
Results may differ from the reference program's by a relative error of at most 0.007.
Values may be sent and summed in bfloat16 or wider, within the bound.
No kernel may reach another device: no remote copies, remote signals or barrier semaphores. Data moves between devices by JAX's collectives and lax.ppermute only.
A program may use at most 64 MiB of HBM per device.

```python
import jax
import jax.numpy as jnp

R = 256
DIMS = 8
PAIRS = 4
N = 262144


def draw_tridiag(key, part):
    key = jax.random.fold_in(key, 7)
    first, second = jax.random.split(key)
    diag = jax.random.uniform(first, (DIMS, R), jnp.float32, 1.0, 1.5)
    offdiag = jax.random.uniform(second, (DIMS, R), jnp.float32, -0.5, 0.5)
    offdiag = offdiag * (jnp.arange(R) < R - 1).astype(jnp.float32)[None, :]
    index = jnp.arange(R)
    eye = index[:, None] == index[None, :]
    above = index[:, None] + 1 == index[None, :]
    below = index[:, None] == index[None, :] + 1
    matrix = jnp.where(eye[None], diag[:, :, None], 0.0)
    matrix = matrix + jnp.where(above[None], offdiag[:, :, None], 0.0)
    matrix = matrix + jnp.where(below[None], offdiag[:, None, :], 0.0)
    return matrix.astype(jnp.bfloat16)


def steps_of(own_key, shape, cuts, low, top_value):
    def one(position, blocks):
        draws = jax.random.uniform(jax.random.fold_in(jax.random.fold_in(own_key, 6), position), (blocks,), jnp.float32, low / len(cuts), top_value / len(cuts))
        return jnp.repeat(jnp.exp(draws), shape[position] // blocks).reshape((-1,) + (1,) * (len(shape) - position - 1))

    level = one(*cuts[0])
    for cut in cuts[1:]:
        level = level * one(*cut)
    return level


def centred(key, extent, width, most, cuts=(), dtype=jnp.bfloat16):
    array = jax.random.normal(key, extent, jnp.float32) * width
    if len(cuts) > 0:
        array = steps_of(key, extent, cuts, -0.22, 0.18) * array
    return jnp.clip(array, min=-most, max=most).astype(dtype)


def setup_inputs(seed: int = 0) -> dict:
    keys = jax.random.split(jax.random.key(seed), 5)
    factors = centred(keys[0], (DIMS, N, R), 1.0, 6.0, ((0, 4), (1, 128)))
    tridiag = draw_tridiag(jax.random.fold_in(keys[4], 71), 0)
    probe_vector = centred(keys[2], (N,), (N ** -0.5), 0.03125, ((0, 128),), jnp.float32)
    cotangent = centred(keys[3], (PAIRS, N), (R ** -0.5), 1.0, ((1, 128),), jnp.float32)
    return {"factors": factors, "tridiag": tridiag, "probe_vector": probe_vector, "cotangent": cotangent}


def reference(factors, tridiag, probe_vector, cotangent):
    lower = []
    upper = []
    for pair in range(PAIRS):
        q_a = factors[pair]
        q_b = factors[pair + PAIRS]
        t_a = tridiag[pair]
        t_b = tridiag[pair + PAIRS]
        c_p = cotangent[pair]
        p_a = jnp.dot(q_a, t_a, preferred_element_type=jnp.float32).astype(jnp.bfloat16)
        p_b = jnp.dot(q_b, t_b, preferred_element_type=jnp.float32).astype(jnp.bfloat16)
        w_p = (probe_vector[:, None] * q_b).astype(jnp.bfloat16)
        u_p = (c_p[:, None] * p_b).astype(jnp.bfloat16)
        m_p = jnp.dot(q_a.T, w_p, preferred_element_type=jnp.float32).astype(jnp.bfloat16)
        g_p = jnp.dot(p_a.T, u_p, preferred_element_type=jnp.float32).astype(jnp.bfloat16)
        e_a = (c_p[:, None] * jnp.dot(p_b, m_p.T, preferred_element_type=jnp.float32)).astype(jnp.bfloat16)
        e_b = (c_p[:, None] * jnp.dot(p_a, m_p, preferred_element_type=jnp.float32)).astype(jnp.bfloat16)
        out_a = jnp.dot(e_a, t_a.T, preferred_element_type=jnp.float32) + probe_vector[:, None] * jnp.dot(q_b, g_p.T, preferred_element_type=jnp.float32)
        out_b = jnp.dot(e_b, t_b.T, preferred_element_type=jnp.float32) + probe_vector[:, None] * jnp.dot(q_a, g_p, preferred_element_type=jnp.float32)
        lower.append(out_a.astype(jnp.bfloat16))
        upper.append(out_b.astype(jnp.bfloat16))
    return jnp.stack(lower + upper, axis=0)
```

```python
import jax
import jax.numpy as jnp
from jax import lax
from jax.experimental import pallas as pl
from jax.experimental.pallas import tpu as pltpu
from jax.sharding import Mesh, PartitionSpec as P

BF = jnp.bfloat16
F32 = jnp.float32
PARAMS = pltpu.CompilerParams(vmem_limit_bytes=40 * 1024 * 1024)
SWAP = [(0, 1), (1, 0)]
REDUCE = ("z1", "xl", "y")
RING = "zh"
SPREAD = ("xh", "z1", "xl", "y")
STEPS = 4


def exchange(x, axes):
    return lax.all_to_all(x, axes, 0, 0, tiled=True)


def prepare(pos, q, t, v, c, left, send0, send1, send2, scale):
    q_own = q[0]
    rows = q_own.shape[0]
    send0[...] = q_own[: rows // 4]
    send1[...] = q_own[rows // 4 : rows // 2]
    send2[...] = q_own[rows // 2 :]
    prod = lax.dot_general(t[0], q_own, (((1,), (1,)), ((), ())), preferred_element_type=F32)
    prod = prod.astype(BF).astype(F32)
    rank = prod.shape[0]
    first = pos[1] * 2
    c_own = c[pl.ds(first + pos[0], 1), :]
    by_v = (prod * v[...]).astype(BF)
    by_c = (prod * c_own).astype(BF)
    width = rows // STEPS
    for k in range(STEPS):
        left[k, :rank] = by_v[:, k * width : (k + 1) * width]
        left[k, rank:] = by_c[:, k * width : (k + 1) * width]
    row = lax.broadcasted_iota(jnp.int32, (128, rows), 0)
    stack = jnp.where(row == 0, v[...], jnp.where(row == 1, c[pl.ds(first, 1), :], c[pl.ds(first + 1, 1), :]))
    scale[...] = stack.T


def gram(pos, left, q, out, acc):
    step = pl.program_id(0)

    @pl.when(step == 0)
    def _():
        acc[...] = jnp.zeros_like(acc)

    acc[...] += jnp.dot(left[0], q[0], preferred_element_type=F32)

    @pl.when(step == STEPS - 1)
    def _():
        parts, kinds, rows, rank = out.shape
        total = acc[...].astype(BF)
        for kind in range(kinds):
            for part in range(parts):
                at = kind * rank + part * rows
                out[part, kind] = total[at : at + rows]


def add_up(x, out):
    total = x[0].astype(F32)
    for k in range(1, x.shape[0]):
        total = total + x[k].astype(F32)
    total = total.astype(BF)
    for k in range(out.shape[0]):
        out[k] = total


def add_up_through(pos, x, t, out):
    total = x[0].astype(F32)
    for k in range(1, x.shape[0]):
        total = total + x[k].astype(F32)
    kinds, rows, rank = total.shape
    flat = total.reshape(kinds * rows, rank)
    high = flat.astype(BF)
    low = (flat - high.astype(F32)).astype(BF)
    res = jnp.dot(high, t[0], preferred_element_type=F32) + jnp.dot(low, t[0], preferred_element_type=F32)
    res = res.astype(BF).reshape(kinds, rows, rank)
    for k in range(out.shape[0]):
        out[k] = res


def finish(pos, mats, q_near, q_far0, q_far1, q_far2, scale, out):
    step = pl.program_id(0)
    near = pos[0]
    far = 1 - near
    slots, parts, kinds, rows, rank = mats.shape
    v = scale[:, 0:1]
    first = scale[:, 1:2]
    second = scale[:, 2:3]
    c_near = jnp.where(near == 0, first, second)
    c_far = jnp.where(near == 0, second, first)

    def pick(slot, kind):
        return mats[slot, :, kind].reshape(parts * rows, rank)

    def across(q, m):
        return lax.dot_general(q, m, (((1,), (1,)), ((), ())), preferred_element_type=F32)

    q = q_near[0]
    res = c_near * across(q, pick(near, 0)) + v * across(q, pick(near, 1))
    out[near] = res.astype(BF)

    def straight(q):
        a = jnp.dot(q, pick(far, 0), preferred_element_type=F32)
        b = jnp.dot(q, pick(far, 1), preferred_element_type=F32)
        out[far] = (c_far * a + v * b).astype(BF)

    @pl.when(step == 0)
    def _():
        straight(q_far0[...])

    @pl.when(step == 1)
    def _():
        straight(q_far1[...])

    @pl.when(step >= 2)
    def _():
        straight(q_far2[...])


def per_device(factors, tridiag, probe_vector, cotangent):
    dims, rows, rank = factors.shape
    quarter = rows // STEPS
    reducers = lax.axis_size(REDUCE)
    ring = lax.axis_size(RING)
    spread = lax.axis_size(SPREAD)
    piece = rank // reducers
    pos = jnp.stack([lax.axis_index("xh"), lax.axis_index("core")]).astype(jnp.int32)
    v = probe_vector.reshape(1, rows)

    met = exchange(factors, "xh")
    left, send0, send1, send2, scale = pl.pallas_call(
        prepare,
        grid_spec=pltpu.PrefetchScalarGridSpec(
            num_scalar_prefetch=1,
            grid=(1,),
            in_specs=[
                pl.BlockSpec((1, rows, rank), lambda i, s: (s[0], 0, 0)),
                pl.BlockSpec((1, rank, rank), lambda i, s: (s[0], 0, 0)),
                pl.BlockSpec((1, rows), lambda i, s: (0, 0)),
                pl.BlockSpec(cotangent.shape, lambda i, s: (0, 0)),
            ],
            out_specs=[
                pl.BlockSpec((STEPS, 2 * rank, quarter), lambda i, s: (0, 0, 0)),
                pl.BlockSpec((quarter, rank), lambda i, s: (0, 0)),
                pl.BlockSpec((quarter, rank), lambda i, s: (0, 0)),
                pl.BlockSpec((2 * quarter, rank), lambda i, s: (0, 0)),
                pl.BlockSpec((rows, 128), lambda i, s: (0, 0)),
            ],
        ),
        out_shape=[
            jax.ShapeDtypeStruct((STEPS, 2 * rank, quarter), BF),
            jax.ShapeDtypeStruct((quarter, rank), BF),
            jax.ShapeDtypeStruct((quarter, rank), BF),
            jax.ShapeDtypeStruct((2 * quarter, rank), BF),
            jax.ShapeDtypeStruct((rows, 128), F32),
        ],
        compiler_params=PARAMS,
        name="prepare",
    )(pos, factors, tridiag, v, cotangent)
    far0 = lax.ppermute(send0, "xh", SWAP)

    part = pl.pallas_call(
        gram,
        grid_spec=pltpu.PrefetchScalarGridSpec(
            num_scalar_prefetch=1,
            grid=(STEPS,),
            in_specs=[
                pl.BlockSpec((1, 2 * rank, quarter), lambda i, s: (i, 0, 0)),
                pl.BlockSpec((1, quarter, rank), lambda i, s: (1 - s[0], i, 0)),
            ],
            out_specs=pl.BlockSpec((reducers, 2, piece, rank), lambda i, s: (0, 0, 0, 0)),
            scratch_shapes=[pltpu.VMEM((2 * rank, rank), F32)],
        ),
        out_shape=jax.ShapeDtypeStruct((reducers, 2, piece, rank), BF),
        compiler_params=PARAMS,
        name="gram",
    )(pos, left, met)
    part, send1, own_t = lax.optimization_barrier((part, send1, tridiag))
    got = exchange(part, REDUCE)
    far1 = lax.ppermute(send1, "xh", SWAP)
    met_t = exchange(own_t, "xh")

    some = pl.pallas_call(
        add_up,
        out_shape=jax.ShapeDtypeStruct((ring, 2, piece, rank), BF),
        compiler_params=PARAMS,
        name="add_up",
    )(got)
    some, send2 = lax.optimization_barrier((some, send2))
    got = exchange(some, RING)
    far2 = lax.ppermute(send2, "xh", SWAP)

    total = pl.pallas_call(
        add_up_through,
        grid_spec=pltpu.PrefetchScalarGridSpec(
            num_scalar_prefetch=1,
            grid=(1,),
            in_specs=[
                pl.BlockSpec((ring, 2, piece, rank), lambda i, s: (0, 0, 0, 0)),
                pl.BlockSpec((1, rank, rank), lambda i, s: (1 - s[0], 0, 0)),
            ],
            out_specs=pl.BlockSpec((spread, 2, piece, rank), lambda i, s: (0, 0, 0, 0)),
        ),
        out_shape=jax.ShapeDtypeStruct((spread, 2, piece, rank), BF),
        compiler_params=PARAMS,
        name="add_up_through",
    )(pos, got, met_t)
    mats = exchange(total, SPREAD).reshape(2, reducers, 2, piece, rank)

    return pl.pallas_call(
        finish,
        grid_spec=pltpu.PrefetchScalarGridSpec(
            num_scalar_prefetch=1,
            grid=(STEPS,),
            in_specs=[
                pl.BlockSpec((2, reducers, 2, piece, rank), lambda i, s: (0, 0, 0, 0, 0)),
                pl.BlockSpec((1, quarter, rank), lambda i, s: (1 - s[0], i, 0)),
                pl.BlockSpec((quarter, rank), lambda i, s: (0, 0)),
                pl.BlockSpec((quarter, rank), lambda i, s: (0, 0)),
                pl.BlockSpec((quarter, rank), lambda i, s: (jnp.maximum(i - 2, 0), 0)),
                pl.BlockSpec((quarter, 128), lambda i, s: (i, 0)),
            ],
            out_specs=pl.BlockSpec((2, quarter, rank), lambda i, s: (0, i, 0)),
        ),
        out_shape=jax.ShapeDtypeStruct((dims, rows, rank), BF),
        compiler_params=PARAMS,
        name="finish",
    )(pos, mats, met, far0, far1, far2, scale)


def solution(mesh):
    pts = mesh.shape["pts"]
    zh = pts // 16
    fine = Mesh(mesh.devices.reshape(2, zh, 2, 4, 2, 2), ("xl", "zh", "z1", "y", "xh", "core"))
    dim = ("xh", "core")
    points = ("xl", "zh", "z1", "y")
    return jax.shard_map(
        per_device,
        mesh=fine,
        in_specs=(P(dim, points, None), P(dim, None, None), P(points), P(None, points)),
        out_specs=P(dim, points, None),
        check_vma=False,
    )
```

```python
import jax
import jax.numpy as jnp
from jax import lax
from jax.experimental import pallas as pl
from jax.experimental.pallas import tpu as pltpu
from jax.sharding import Mesh, PartitionSpec as P

BF = jnp.bfloat16
F32 = jnp.float32
PARAMS = pltpu.CompilerParams(vmem_limit_bytes=24 * 1024 * 1024)
SWAP = [(0, 1), (1, 0)]
REDUCE = ("z1", "xl", "y")
RING = "zh"
SPREAD = ("xh", "z1", "xl", "y")
STEPS = 4
ANY = pl.BlockSpec(memory_space=pl.ANY)
HBM = pl.BlockSpec(memory_space=pltpu.HBM)
SMEM = pl.BlockSpec(memory_space=pltpu.SMEM)
VMEM = pl.BlockSpec(memory_space=pltpu.VMEM)


def like(x):
    return jax.ShapeDtypeStruct(x.shape, x.dtype)


def exchange(x, axes):
    return lax.all_to_all(x, axes, 0, 0, tiled=True)


def prepare(pos, q, t, v, c, prod, weights, send, scale, bands):
    step = pl.program_id(0)
    q_own = q[0]
    rows, rank = q_own.shape

    @pl.when(step == 0)
    def _():
        row = lax.broadcasted_iota(jnp.int32, (rank, rank), 0)
        column = lax.broadcasted_iota(jnp.int32, (rank, rank), 1)
        line = lax.broadcasted_iota(jnp.int32, bands.shape, 0)
        full = t[1 - pos[0]].astype(F32)
        band = jnp.zeros(bands.shape, F32)
        for k in range(3):
            entries = jnp.sum(jnp.where(row == column + (k - 1), full, 0.0), axis=0, keepdims=True)
            band = jnp.where(line == k, entries, band)
        bands[...] = band.astype(BF)

    send[...] = q_own
    own = lax.dot_general(t[pos[0]], q_own, (((1,), (1,)), ((), ())), preferred_element_type=F32)
    prod[0] = own.astype(BF)
    c_near = c[pl.ds(pos[1] * 2 + pos[0], 1), :]
    c_far = c[pl.ds(pos[1] * 2 + 1 - pos[0], 1), :]
    line = lax.broadcasted_iota(jnp.int32, weights.shape[1:], 0)
    weights[0] = jnp.where(line == 0, v[...], c_near)
    row = lax.broadcasted_iota(jnp.int32, (128, rows), 0)
    scale[...] = jnp.where(row == 0, v[...], jnp.where(row == 1, c_near, c_far)).T


def gram(pos, prod, weights, q, bands, send, out, sent, prod_here, weights_here, sems):
    del bands, send, sent
    parts, kinds, rows, rank = out.shape
    copies = [pltpu.make_async_copy(weights, weights_here, sems.at[STEPS])]
    copies += [pltpu.make_async_copy(prod.at[k], prod_here.at[k], sems.at[k]) for k in range(STEPS)]
    for copy in copies:
        copy.start()
    copies[0].wait()
    left = []
    for k in range(STEPS):
        copies[k + 1].wait()
        block = prod_here[k].astype(F32)
        left.append(jnp.concatenate([(block * weights_here[k, n : n + 1]).astype(BF) for n in range(kinds)], axis=0))
    total = jnp.dot(jnp.concatenate(left, axis=1), q[1 - pos[0]], preferred_element_type=F32)
    total = total.astype(BF)
    for kind in range(kinds):
        for part in range(parts):
            at = kind * rank + part * rows
            out[part, kind] = total[at : at + rows]


def total_of(x):
    total = x[0].astype(F32)
    for k in range(1, x.shape[0]):
        total = total + x[k].astype(F32)
    return total


def add_up(x, out):
    total = total_of(x).astype(BF)
    for k in range(out.shape[0]):
        out[k] = total


def add_up_through(x, bands, far, out):
    del far
    total = total_of(x)
    kinds, rows, rank = total.shape
    flat = total.reshape(kinds * rows, rank)
    band = bands[...].astype(F32)
    res = flat * band[1:2] + pltpu.roll(flat, 1, 1) * band[0:1] + pltpu.roll(flat, rank - 1, 1) * band[2:3]
    res = res.astype(BF).reshape(kinds, rows, rank)
    for k in range(out.shape[0]):
        out[k] = res


def finish(pos, mats, q_near, q_far, scale, out, here, sems):
    near = pos[0]
    slots, parts, kinds, rows, rank = mats.shape
    width = here.shape[2]

    def pick(slot, kind):
        return mats[slot, :, kind].reshape(parts * rows, rank)

    def across(q, m):
        return lax.dot_general(q, m, (((1,), (1,)), ((), ())), preferred_element_type=F32)

    def straight(q, m):
        return jnp.dot(q, m, preferred_element_type=F32)

    copies = []
    for which, slot, multiply in ((0, near, across), (1, 1 - near, straight)):
        by_c = pick(slot, 0)
        by_v = pick(slot, 1)
        for k in range(STEPS):
            span = pl.ds(k * width, width)
            q = q_near[1 - near, span] if which == 0 else q_far[span]
            res = scale[span, 1 + which : 2 + which] * multiply(q, by_c) + scale[span, 0:1] * multiply(q, by_v)
            here[which, k] = res.astype(BF)
            copy = pltpu.make_async_copy(here.at[which, k], out.at[slot, span], sems.at[which, k])
            copy.start()
            copies.append(copy)
    for copy in copies:
        copy.wait()


def per_device(factors, tridiag, probe_vector, cotangent):
    dims, rows, rank = factors.shape
    quarter = rows // STEPS
    reducers = lax.axis_size(REDUCE)
    ring = lax.axis_size(RING)
    spread = lax.axis_size(SPREAD)
    piece = rank // reducers
    pos = jnp.stack([lax.axis_index("xh"), lax.axis_index("core")]).astype(jnp.int32)
    v = probe_vector.reshape(1, rows)

    met = exchange(factors, "xh")
    prod, weights, send, scale, bands = pl.pallas_call(
        prepare,
        grid_spec=pltpu.PrefetchScalarGridSpec(
            num_scalar_prefetch=1,
            grid=(STEPS,),
            in_specs=[
                pl.BlockSpec((1, quarter, rank), lambda i, s: (s[0], i, 0)),
                pl.BlockSpec((dims, rank, rank), lambda i, s: (0, 0, 0)),
                pl.BlockSpec((1, quarter), lambda i, s: (0, i)),
                pl.BlockSpec((cotangent.shape[0], quarter), lambda i, s: (0, i)),
            ],
            out_specs=[
                pl.BlockSpec((1, rank, quarter), lambda i, s: (i, 0, 0)),
                pl.BlockSpec((1, 8, quarter), lambda i, s: (i, 0, 0)),
                pl.BlockSpec((quarter, rank), lambda i, s: (i, 0)),
                pl.BlockSpec((quarter, 128), lambda i, s: (i, 0)),
                pl.BlockSpec((16, rank), lambda i, s: (0, 0)),
            ],
        ),
        out_shape=[
            jax.ShapeDtypeStruct((STEPS, rank, quarter), BF),
            jax.ShapeDtypeStruct((STEPS, 8, quarter), F32),
            jax.ShapeDtypeStruct((rows, rank), BF),
            jax.ShapeDtypeStruct((rows, 128), F32),
            jax.ShapeDtypeStruct((16, rank), BF),
        ],
        compiler_params=PARAMS,
        name="prepare",
    )(pos, factors, tridiag, v, cotangent)
    bands = lax.ppermute(bands, "xh", SWAP)

    part, send = pl.pallas_call(
        gram,
        in_specs=[SMEM, HBM, HBM, VMEM, ANY, ANY],
        out_specs=[VMEM, ANY],
        out_shape=[jax.ShapeDtypeStruct((reducers, 2, piece, rank), BF), like(send)],
        scratch_shapes=[
            pltpu.VMEM(prod.shape, BF),
            pltpu.VMEM(weights.shape, F32),
            pltpu.SemaphoreType.DMA((STEPS + 1,)),
        ],
        input_output_aliases={5: 1},
        compiler_params=PARAMS,
        name="gram",
    )(pos, prod, weights, met, bands, send)
    got = exchange(part, REDUCE)
    far = lax.ppermute(send, "xh", SWAP)

    some = pl.pallas_call(
        add_up,
        in_specs=[VMEM],
        out_specs=VMEM,
        out_shape=jax.ShapeDtypeStruct((ring, 2, piece, rank), BF),
        compiler_params=PARAMS,
        name="add_up",
    )(got)
    got = exchange(some, RING)

    total = pl.pallas_call(
        add_up_through,
        in_specs=[VMEM, VMEM, ANY],
        out_specs=VMEM,
        out_shape=jax.ShapeDtypeStruct((spread, 2, piece, rank), BF),
        compiler_params=PARAMS,
        name="add_up_through",
    )(got, bands, far)
    mats = exchange(total, SPREAD).reshape(2, reducers, 2, piece, rank)

    return pl.pallas_call(
        finish,
        in_specs=[SMEM, VMEM, VMEM, VMEM, VMEM],
        out_specs=HBM,
        out_shape=jax.ShapeDtypeStruct((dims, rows, rank), BF),
        scratch_shapes=[pltpu.VMEM((2, STEPS, quarter, rank), BF), pltpu.SemaphoreType.DMA((2, STEPS))],
        compiler_params=PARAMS,
        name="finish",
    )(pos, mats, met, far, scale)


def solution(mesh):
    pts = mesh.shape["pts"]
    zh = pts // 16
    fine = Mesh(mesh.devices.reshape(2, zh, 2, 4, 2, 2), ("xl", "zh", "z1", "y", "xh", "core"))
    dim = ("xh", "core")
    points = ("xl", "zh", "z1", "y")
    return jax.shard_map(
        per_device,
        mesh=fine,
        in_specs=(P(dim, points, None), P(dim, None, None), P(points), P(None, points)),
        out_specs=P(dim, points, None),
        check_vma=False,
    )
```

```python
import jax
import jax.numpy as jnp
from jax import lax
from jax.experimental import pallas as pl
from jax.experimental.pallas import tpu as pltpu
from jax.sharding import Mesh, PartitionSpec as P

BF = jnp.bfloat16
F32 = jnp.float32
PARAMS = pltpu.CompilerParams(vmem_limit_bytes=24 * 1024 * 1024)
SWAP = [(0, 1), (1, 0)]
REDUCE = ("z1", "xl", "y")
RING = "zh"
SPREAD = ("xh", "z1", "xl", "y")
STEPS = 4
ANY = pl.BlockSpec(memory_space=pl.ANY)
HBM = pl.BlockSpec(memory_space=pltpu.HBM)
SMEM = pl.BlockSpec(memory_space=pltpu.SMEM)
VMEM = pl.BlockSpec(memory_space=pltpu.VMEM)


def like(x):
    return jax.ShapeDtypeStruct(x.shape, x.dtype)


def exchange(x, axes, order=None):
    groups = None if order is None else [order]
    return lax.all_to_all(x, axes, 0, 0, tiled=True, axis_index_groups=groups)


def prepare(pos, q, t, v, c, prod, weights, send, bands):
    step = pl.program_id(0)
    q_own = q[0]
    rows, rank = q_own.shape

    @pl.when(step == 0)
    def _():
        row = lax.broadcasted_iota(jnp.int32, (rank, rank), 0)
        column = lax.broadcasted_iota(jnp.int32, (rank, rank), 1)
        line = lax.broadcasted_iota(jnp.int32, bands.shape, 0)
        full = t[1 - pos[0]].astype(F32)
        band = jnp.zeros(bands.shape, F32)
        for k in range(3):
            entries = jnp.sum(jnp.where(row == column + (k - 1), full, 0.0), axis=0, keepdims=True)
            band = jnp.where(line == k, entries, band)
        bands[...] = band.astype(BF)

    send[...] = q_own
    own = lax.dot_general(t[pos[0]], q_own, (((1,), (1,)), ((), ())), preferred_element_type=F32)
    prod[0] = own.astype(BF)
    c_near = c[pl.ds(pos[1] * 2 + pos[0], 1), :]
    c_far = c[pl.ds(pos[1] * 2 + 1 - pos[0], 1), :]
    line = lax.broadcasted_iota(jnp.int32, weights.shape[1:], 0)
    weights[0] = jnp.where(line == 0, v[...], jnp.where(line == 1, c_near, c_far))


def gram(pos, prod, weights, q, bands, out, here, sem):
    del bands
    parts, kinds, rows, rank = out.shape
    left = []
    for k in range(STEPS):
        block = prod[k].astype(F32)
        left.append(jnp.concatenate([(block * weights[k, n : n + 1]).astype(BF) for n in range(kinds)], axis=0))
    total = jnp.dot(jnp.concatenate(left, axis=1), q[1 - pos[0]], preferred_element_type=F32)
    total = total.astype(BF)
    for kind in range(kinds):
        for part in range(parts):
            at = kind * rank + part * rows
            here[part, kind] = total[at : at + rows]
    copy = pltpu.make_async_copy(here, out, sem)
    copy.start()
    copy.wait()


def total_of(x):
    total = x[0].astype(F32)
    for k in range(1, x.shape[0]):
        total = total + x[k].astype(F32)
    return total


def add_up(x, out):
    total = total_of(x).astype(BF)
    for k in range(out.shape[0]):
        out[k] = total


def add_up_through(x, bands, far, out):
    del far
    total = total_of(x)
    kinds, rows, rank = total.shape
    flat = total.reshape(kinds * rows, rank)
    band = bands[...].astype(F32)
    res = flat * band[1:2] + pltpu.roll(flat, 1, 1) * band[0:1] + pltpu.roll(flat, rank - 1, 1) * band[2:3]
    res = res.astype(BF).reshape(kinds, rows, rank)
    for k in range(out.shape[0]):
        out[k] = res


def finish(pos, mats, q_near, q_far, weights, out, here, sems):
    near = pos[0]
    slots, parts, kinds, rows, rank = mats.shape
    width = here.shape[2]

    def pick(slot, kind):
        return mats[1 - slot, :, kind].reshape(parts * rows, rank)

    def across(q, m):
        return lax.dot_general(q, m, (((1,), (1,)), ((), ())), preferred_element_type=F32)

    def straight(q, m):
        return jnp.dot(q, m, preferred_element_type=F32)

    def column(k, n):
        return jnp.concatenate([jnp.broadcast_to(weights[k, n : n + 1], (128, width)).T] * (rank // 128), axis=1)

    def far_block(k):
        block = q_far[k * width : min((k + 1) * width, q_far.shape[0])]
        return block

    copies = []
    for which, slot, multiply in ((0, near, across), (1, 1 - near, straight)):
        by_c = pick(slot, 0)
        by_v = pick(slot, 1)
        for k in range(STEPS):
            span = pl.ds(k * width, width)
            q = q_near[1 - near, span] if which == 0 else far_block(k)
            res = column(k, 1 + which) * multiply(q, by_c) + column(k, 0) * multiply(q, by_v)
            here[which, k] = res.astype(BF)
            copy = pltpu.make_async_copy(here.at[which, k], out.at[slot, span], sems.at[which, k])
            copy.start()
            copies.append(copy)
    for copy in copies:
        copy.wait()


def per_device(factors, tridiag, probe_vector, cotangent):
    dims, rows, rank = factors.shape
    quarter = rows // STEPS
    reducers = lax.axis_size(REDUCE)
    ring = lax.axis_size(RING)
    spread = lax.axis_size(SPREAD)
    piece = rank // reducers
    pos = jnp.stack([lax.axis_index("xh"), lax.axis_index("core")]).astype(jnp.int32)
    v = probe_vector.reshape(1, rows)

    met = exchange(factors, "xh")
    prod, weights, send, bands = pl.pallas_call(
        prepare,
        grid_spec=pltpu.PrefetchScalarGridSpec(
            num_scalar_prefetch=1,
            grid=(STEPS,),
            in_specs=[
                pl.BlockSpec((1, quarter, rank), lambda i, s: (s[0], i, 0)),
                pl.BlockSpec((dims, rank, rank), lambda i, s: (0, 0, 0)),
                pl.BlockSpec((1, quarter), lambda i, s: (0, i)),
                pl.BlockSpec((cotangent.shape[0], quarter), lambda i, s: (0, i)),
            ],
            out_specs=[
                pl.BlockSpec((1, rank, quarter), lambda i, s: (i, 0, 0)),
                pl.BlockSpec((1, 8, quarter), lambda i, s: (i, 0, 0)),
                pl.BlockSpec((quarter, rank), lambda i, s: (i, 0)),
                pl.BlockSpec((16, rank), lambda i, s: (0, 0)),
            ],
        ),
        out_shape=[
            jax.ShapeDtypeStruct((STEPS, rank, quarter), BF),
            jax.ShapeDtypeStruct((STEPS, 8, quarter), F32),
            jax.ShapeDtypeStruct((rows, rank), BF),
            jax.ShapeDtypeStruct((16, rank), BF),
        ],
        compiler_params=PARAMS,
        name="prepare",
    )(pos, factors, tridiag, v, cotangent)
    bands = lax.ppermute(bands, "xh", SWAP)

    part = pl.pallas_call(
        gram,
        in_specs=[SMEM, VMEM, VMEM, VMEM, ANY],
        out_specs=ANY,
        out_shape=jax.ShapeDtypeStruct((reducers, 2, piece, rank), BF),
        scratch_shapes=[pltpu.VMEM((reducers, 2, piece, rank), BF), pltpu.SemaphoreType.DMA(())],
        compiler_params=PARAMS,
        name="gram",
    )(pos, prod, weights, met, bands)
    got = exchange(part, REDUCE, list(range(reducers))[::-1])
    far = lax.ppermute(send, "xh", SWAP)

    some = pl.pallas_call(
        add_up,
        in_specs=[VMEM],
        out_specs=VMEM,
        out_shape=jax.ShapeDtypeStruct((ring, 2, piece, rank), BF),
        compiler_params=PARAMS,
        name="add_up",
    )(got)
    got = exchange(some, RING, [(k + ring // 2) % ring for k in range(ring)])

    total = pl.pallas_call(
        add_up_through,
        in_specs=[VMEM, VMEM, ANY],
        out_specs=VMEM,
        out_shape=jax.ShapeDtypeStruct((spread, 2, piece, rank), BF),
        compiler_params=PARAMS,
        name="add_up_through",
    )(got, bands, far)
    mats = exchange(total, SPREAD, list(range(spread))[::-1]).reshape(2, reducers, 2, piece, rank)

    return pl.pallas_call(
        finish,
        in_specs=[SMEM, VMEM, VMEM, VMEM, VMEM],
        out_specs=HBM,
        out_shape=jax.ShapeDtypeStruct((dims, rows, rank), BF),
        scratch_shapes=[pltpu.VMEM((2, STEPS, quarter, rank), BF), pltpu.SemaphoreType.DMA((2, STEPS))],
        compiler_params=PARAMS,
        name="finish",
    )(pos, mats, met, far, weights)


def solution(mesh):
    pts = mesh.shape["pts"]
    zh = pts // 16
    fine = Mesh(mesh.devices.reshape(2, zh, 2, 4, 2, 2), ("xl", "zh", "z1", "y", "xh", "core"))
    dim = ("xh", "core")
    points = ("xl", "zh", "z1", "y")
    return jax.shard_map(
        per_device,
        mesh=fine,
        in_specs=(P(dim, points, None), P(dim, None, None), P(points), P(None, points)),
        out_specs=P(dim, points, None),
        check_vma=False,
    )
```

```python
import jax
import jax.numpy as jnp
from jax import lax
from jax.experimental import pallas as pl
from jax.experimental.pallas import tpu as pltpu
from jax.sharding import Mesh, PartitionSpec as P

BF = jnp.bfloat16
F32 = jnp.float32
PARAMS = pltpu.CompilerParams(vmem_limit_bytes=24 * 1024 * 1024)
SWAP = [(0, 1), (1, 0)]
REDUCE = ("z1", "xl", "y")
RING = "zh"
SPREAD = ("xh", "z1", "xl", "y")
STEPS = 4
ANY = pl.BlockSpec(memory_space=pl.ANY)
HBM = pl.BlockSpec(memory_space=pltpu.HBM)
SMEM = pl.BlockSpec(memory_space=pltpu.SMEM)
VMEM = pl.BlockSpec(memory_space=pltpu.VMEM)


def like(x):
    return jax.ShapeDtypeStruct(x.shape, x.dtype)


def exchange(x, axes, order=None):
    groups = None if order is None else [order]
    return lax.all_to_all(x, axes, 0, 0, tiled=True, axis_index_groups=groups)


def prepare(pos, q, t, v, c, prod, weights, send, bands):
    step = pl.program_id(0)
    q_own = q[0]
    rows, rank = q_own.shape

    @pl.when(step == 0)
    def _():
        row = lax.broadcasted_iota(jnp.int32, (rank, rank), 0)
        column = lax.broadcasted_iota(jnp.int32, (rank, rank), 1)
        line = lax.broadcasted_iota(jnp.int32, bands.shape, 0)
        full = t[1 - pos[0]].astype(F32)
        band = jnp.zeros(bands.shape, F32)
        for k in range(3):
            entries = jnp.sum(jnp.where(row == column + (k - 1), full, 0.0), axis=0, keepdims=True)
            band = jnp.where(line == k, entries, band)
        bands[...] = band.astype(BF)

    send[...] = q_own
    own = lax.dot_general(t[pos[0]], q_own, (((1,), (1,)), ((), ())), preferred_element_type=F32)
    prod[0] = own.astype(BF)
    c_near = c[pl.ds(pos[1] * 2 + pos[0], 1), :]
    c_far = c[pl.ds(pos[1] * 2 + 1 - pos[0], 1), :]
    line = lax.broadcasted_iota(jnp.int32, weights.shape[1:], 0)
    weights[0] = jnp.where(line == 0, v[...], jnp.where(line == 1, c_near, c_far))


def gram(pos, prod, weights, q, bands, out, here, sem):
    del bands
    parts, kinds, rows, rank = out.shape
    left = []
    for k in range(STEPS):
        block = prod[k].astype(F32)
        left.append(jnp.concatenate([(block * weights[k, n : n + 1]).astype(BF) for n in range(kinds)], axis=0))
    total = jnp.dot(jnp.concatenate(left, axis=1), q[1 - pos[0]], preferred_element_type=F32)
    total = total.astype(BF)
    for kind in range(kinds):
        for part in range(parts):
            at = kind * rank + part * rows
            here[part, kind] = total[at : at + rows]
    copy = pltpu.make_async_copy(here, out, sem)
    copy.start()
    copy.wait()


def hold(x, after, same):
    del x, after, same


def total_of(x):
    total = x[0].astype(F32)
    for k in range(1, x.shape[0]):
        total = total + x[k].astype(F32)
    return total


def add_up(x, out):
    total = total_of(x).astype(BF)
    for k in range(out.shape[0]):
        out[k] = total


def add_up_through(x, bands, out):
    total = total_of(x)
    kinds, rows, rank = total.shape
    flat = total.reshape(kinds * rows, rank)
    band = bands[...].astype(F32)
    res = flat * band[1:2] + pltpu.roll(flat, 1, 1) * band[0:1] + pltpu.roll(flat, rank - 1, 1) * band[2:3]
    res = res.astype(BF).reshape(kinds, rows, rank)
    for k in range(out.shape[0]):
        out[k] = res


def finish(pos, mats, q_near, q_far, weights, out, here, sems):
    near = pos[0]
    slots, parts, kinds, rows, rank = mats.shape
    width = here.shape[2]

    def pick(slot, kind):
        return mats[1 - slot, :, kind].reshape(parts * rows, rank)

    def across(q, m):
        return lax.dot_general(q, m, (((1,), (1,)), ((), ())), preferred_element_type=F32)

    def straight(q, m):
        return jnp.dot(q, m, preferred_element_type=F32)

    def column(k, n):
        return jnp.concatenate([jnp.broadcast_to(weights[k, n : n + 1], (128, width)).T] * (rank // 128), axis=1)

    def far_block(k):
        block = q_far[k * width : min((k + 1) * width, q_far.shape[0])]
        return block

    copies = []
    for which, slot, multiply in ((0, near, across), (1, 1 - near, straight)):
        by_c = pick(slot, 0)
        by_v = pick(slot, 1)
        for k in range(STEPS):
            span = pl.ds(k * width, width)
            q = q_near[1 - near, span] if which == 0 else far_block(k)
            res = column(k, 1 + which) * multiply(q, by_c) + column(k, 0) * multiply(q, by_v)
            here[which, k] = res.astype(BF)
            copy = pltpu.make_async_copy(here.at[which, k], out.at[slot, span], sems.at[which, k])
            copy.start()
            copies.append(copy)
    for copy in copies:
        copy.wait()


def per_device(factors, tridiag, probe_vector, cotangent):
    dims, rows, rank = factors.shape
    quarter = rows // STEPS
    reducers = lax.axis_size(REDUCE)
    ring = lax.axis_size(RING)
    spread = lax.axis_size(SPREAD)
    piece = rank // reducers
    pos = jnp.stack([lax.axis_index("xh"), lax.axis_index("core")]).astype(jnp.int32)
    v = probe_vector.reshape(1, rows)

    met = exchange(factors, "xh")
    prod, weights, send, bands = pl.pallas_call(
        prepare,
        grid_spec=pltpu.PrefetchScalarGridSpec(
            num_scalar_prefetch=1,
            grid=(STEPS,),
            in_specs=[
                pl.BlockSpec((1, quarter, rank), lambda i, s: (s[0], i, 0)),
                pl.BlockSpec((dims, rank, rank), lambda i, s: (0, 0, 0)),
                pl.BlockSpec((1, quarter), lambda i, s: (0, i)),
                pl.BlockSpec((cotangent.shape[0], quarter), lambda i, s: (0, i)),
            ],
            out_specs=[
                pl.BlockSpec((1, rank, quarter), lambda i, s: (i, 0, 0)),
                pl.BlockSpec((1, 8, quarter), lambda i, s: (i, 0, 0)),
                pl.BlockSpec((quarter, rank), lambda i, s: (i, 0)),
                pl.BlockSpec((16, rank), lambda i, s: (0, 0)),
            ],
        ),
        out_shape=[
            jax.ShapeDtypeStruct((STEPS, rank, quarter), BF),
            jax.ShapeDtypeStruct((STEPS, 8, quarter), F32),
            jax.ShapeDtypeStruct((rows, rank), BF),
            jax.ShapeDtypeStruct((16, rank), BF),
        ],
        compiler_params=PARAMS,
        name="prepare",
    )(pos, factors, tridiag, v, cotangent)
    bands = lax.ppermute(bands, "xh", SWAP)

    part = pl.pallas_call(
        gram,
        in_specs=[SMEM, VMEM, VMEM, VMEM, ANY],
        out_specs=ANY,
        out_shape=jax.ShapeDtypeStruct((reducers, 2, piece, rank), BF),
        scratch_shapes=[pltpu.VMEM((reducers, 2, piece, rank), BF), pltpu.SemaphoreType.DMA(())],
        compiler_params=PARAMS,
        name="gram",
    )(pos, prod, weights, met, bands)
    got = exchange(part, REDUCE, list(range(reducers))[::-1])
    far = lax.ppermute(send, "xh", SWAP)

    some = pl.pallas_call(
        add_up,
        in_specs=[VMEM],
        out_specs=VMEM,
        out_shape=jax.ShapeDtypeStruct((ring, 2, piece, rank), BF),
        compiler_params=PARAMS,
        name="add_up",
    )(got)
    got = exchange(some, RING, [(k + ring // 2) % ring for k in range(ring)])

    total = pl.pallas_call(
        add_up_through,
        in_specs=[VMEM, VMEM],
        out_specs=VMEM,
        out_shape=jax.ShapeDtypeStruct((spread, 2, piece, rank), BF),
        compiler_params=PARAMS,
        name="add_up_through",
    )(got, bands)
    total = pl.pallas_call(
        hold,
        in_specs=[ANY, ANY],
        out_specs=ANY,
        out_shape=like(total),
        input_output_aliases={0: 0},
        compiler_params=PARAMS,
        name="hold",
    )(total, far)
    mats = exchange(total, SPREAD, list(range(spread))[::-1]).reshape(2, reducers, 2, piece, rank)

    return pl.pallas_call(
        finish,
        in_specs=[SMEM, VMEM, VMEM, VMEM, VMEM],
        out_specs=HBM,
        out_shape=jax.ShapeDtypeStruct((dims, rows, rank), BF),
        scratch_shapes=[pltpu.VMEM((2, STEPS, quarter, rank), BF), pltpu.SemaphoreType.DMA((2, STEPS))],
        compiler_params=PARAMS,
        name="finish",
    )(pos, mats, met, far, weights)


def solution(mesh):
    pts = mesh.shape["pts"]
    zh = pts // 16
    fine = Mesh(mesh.devices.reshape(2, zh, 2, 4, 2, 2), ("xl", "zh", "z1", "y", "xh", "core"))
    dim = ("xh", "core")
    points = ("xl", "zh", "z1", "y")
    return jax.shard_map(
        per_device,
        mesh=fine,
        in_specs=(P(dim, points, None), P(dim, None, None), P(points), P(None, points)),
        out_specs=P(dim, points, None),
        check_vma=False,
    )
```

```python
import jax
import jax.numpy as jnp
from jax import lax
from jax.experimental import pallas as pl
from jax.experimental.pallas import tpu as pltpu
from jax.sharding import Mesh, PartitionSpec as P

BF = jnp.bfloat16
F32 = jnp.float32
PARAMS = pltpu.CompilerParams(vmem_limit_bytes=24 * 1024 * 1024)
SWAP = [(0, 1), (1, 0)]
REDUCE = ("z1", "xl", "y")
RING = "zh"
SPREAD = ("xh", "z1", "xl", "y")
STEPS = 4
ANY = pl.BlockSpec(memory_space=pl.ANY)
HBM = pl.BlockSpec(memory_space=pltpu.HBM)
SMEM = pl.BlockSpec(memory_space=pltpu.SMEM)
VMEM = pl.BlockSpec(memory_space=pltpu.VMEM)


def like(x):
    return jax.ShapeDtypeStruct(x.shape, x.dtype)


def exchange(x, axes, order=None):
    groups = None if order is None else [order]
    return lax.all_to_all(x, axes, 0, 0, tiled=True, axis_index_groups=groups)


def prepare(pos, q, t, v, c, prod, weights, send, bands):
    step = pl.program_id(0)
    q_own = q[0]
    rows, rank = q_own.shape

    @pl.when(step == 0)
    def _():
        row = lax.broadcasted_iota(jnp.int32, (rank, rank), 0)
        column = lax.broadcasted_iota(jnp.int32, (rank, rank), 1)
        line = lax.broadcasted_iota(jnp.int32, bands.shape, 0)
        full = t[1 - pos[0]].astype(F32)
        band = jnp.zeros(bands.shape, F32)
        for k in range(3):
            entries = jnp.sum(jnp.where(row == column + (k - 1), full, 0.0), axis=0, keepdims=True)
            band = jnp.where(line == k, entries, band)
        bands[...] = band.astype(BF)

    send[...] = q_own
    own = lax.dot_general(t[pos[0]], q_own, (((1,), (1,)), ((), ())), preferred_element_type=F32)
    prod[0] = own.astype(BF)
    c_near = c[pl.ds(pos[1] * 2 + pos[0], 1), :]
    c_far = c[pl.ds(pos[1] * 2 + 1 - pos[0], 1), :]
    line = lax.broadcasted_iota(jnp.int32, weights.shape[1:], 0)
    weights[0] = jnp.where(line == 0, v[...], jnp.where(line == 1, c_near, c_far))


def gram(pos, prod, weights, q, bands, out, here, sem):
    del bands
    parts, kinds, rows, rank = out.shape
    left = []
    for k in range(STEPS):
        left.append(jnp.concatenate([prod[k] * weights[k, n : n + 1].astype(BF) for n in range(kinds)], axis=0))
    total = jnp.dot(jnp.concatenate(left, axis=1), q[1 - pos[0]], preferred_element_type=F32)
    total = total.astype(BF)
    for kind in range(kinds):
        for part in range(parts):
            at = kind * rank + part * rows
            here[part, kind] = total[at : at + rows]
    copy = pltpu.make_async_copy(here, out, sem)
    copy.start()
    copy.wait()


def hold(x, after, same):
    del x, after, same


def total_of(x):
    total = x[0].astype(F32)
    for k in range(1, x.shape[0]):
        total = total + x[k].astype(F32)
    return total


def add_up(x, out):
    total = total_of(x).astype(BF)
    for k in range(out.shape[0]):
        out[k] = total


def add_up_through(x, bands, out):
    total = total_of(x)
    kinds, rows, rank = total.shape
    flat = total.reshape(kinds * rows, rank)
    band = bands[...].astype(F32)
    res = flat * band[1:2] + pltpu.roll(flat, 1, 1) * band[0:1] + pltpu.roll(flat, rank - 1, 1) * band[2:3]
    res = res.astype(BF).reshape(kinds, rows, rank)
    for k in range(out.shape[0]):
        out[k] = res


def finish(pos, mats, q_near, q_far, weights, out, here, sems):
    near = pos[0]
    slots, parts, kinds, rows, rank = mats.shape
    width = here.shape[2]

    def pick(slot, kind):
        return mats[1 - slot, :, kind].reshape(parts * rows, rank)

    def across(q, m):
        return lax.dot_general(q, m, (((1,), (1,)), ((), ())), preferred_element_type=F32)

    def straight(q, m):
        return jnp.dot(q, m, preferred_element_type=F32)

    def column(k, n):
        return jnp.concatenate([jnp.broadcast_to(weights[k, n : n + 1], (128, width)).T] * (rank // 128), axis=1)

    def far_block(k):
        block = q_far[k * width : min((k + 1) * width, q_far.shape[0])]
        return block

    copies = []
    for which, slot, multiply in ((0, near, across), (1, 1 - near, straight)):
        by_c = pick(slot, 0)
        by_v = pick(slot, 1)
        for k in range(STEPS):
            span = pl.ds(k * width, width)
            q = q_near[1 - near, span] if which == 0 else far_block(k)
            res = column(k, 1 + which) * multiply(q, by_c) + column(k, 0) * multiply(q, by_v)
            here[which, k] = res.astype(BF)
            copy = pltpu.make_async_copy(here.at[which, k], out.at[slot, span], sems.at[which, k])
            copy.start()
            copies.append(copy)
    for copy in copies:
        copy.wait()


def per_device(factors, tridiag, probe_vector, cotangent):
    dims, rows, rank = factors.shape
    quarter = rows // STEPS
    reducers = lax.axis_size(REDUCE)
    ring = lax.axis_size(RING)
    spread = lax.axis_size(SPREAD)
    piece = rank // reducers
    pos = jnp.stack([lax.axis_index("xh"), lax.axis_index("core")]).astype(jnp.int32)
    v = probe_vector.reshape(1, rows)

    met = exchange(factors, "xh")
    prod, weights, send, bands = pl.pallas_call(
        prepare,
        grid_spec=pltpu.PrefetchScalarGridSpec(
            num_scalar_prefetch=1,
            grid=(STEPS,),
            in_specs=[
                pl.BlockSpec((1, quarter, rank), lambda i, s: (s[0], i, 0)),
                pl.BlockSpec((dims, rank, rank), lambda i, s: (0, 0, 0)),
                pl.BlockSpec((1, quarter), lambda i, s: (0, i)),
                pl.BlockSpec((cotangent.shape[0], quarter), lambda i, s: (0, i)),
            ],
            out_specs=[
                pl.BlockSpec((1, rank, quarter), lambda i, s: (i, 0, 0)),
                pl.BlockSpec((1, 8, quarter), lambda i, s: (i, 0, 0)),
                pl.BlockSpec((quarter, rank), lambda i, s: (i, 0)),
                pl.BlockSpec((16, rank), lambda i, s: (0, 0)),
            ],
        ),
        out_shape=[
            jax.ShapeDtypeStruct((STEPS, rank, quarter), BF),
            jax.ShapeDtypeStruct((STEPS, 8, quarter), F32),
            jax.ShapeDtypeStruct((rows, rank), BF),
            jax.ShapeDtypeStruct((16, rank), BF),
        ],
        compiler_params=PARAMS,
        name="prepare",
    )(pos, factors, tridiag, v, cotangent)
    bands = lax.ppermute(bands, "xh", SWAP)

    part = pl.pallas_call(
        gram,
        in_specs=[SMEM, VMEM, VMEM, VMEM, ANY],
        out_specs=ANY,
        out_shape=jax.ShapeDtypeStruct((reducers, 2, piece, rank), BF),
        scratch_shapes=[pltpu.VMEM((reducers, 2, piece, rank), BF), pltpu.SemaphoreType.DMA(())],
        compiler_params=PARAMS,
        name="gram",
    )(pos, prod, weights, met, bands)
    got = exchange(part, REDUCE, list(range(reducers))[::-1])
    far = lax.ppermute(send, "xh", SWAP)

    some = pl.pallas_call(
        add_up,
        in_specs=[VMEM],
        out_specs=VMEM,
        out_shape=jax.ShapeDtypeStruct((ring, 2, piece, rank), BF),
        compiler_params=PARAMS,
        name="add_up",
    )(got)
    got = exchange(some, RING, [(k + ring // 2) % ring for k in range(ring)])

    total = pl.pallas_call(
        add_up_through,
        in_specs=[VMEM, VMEM],
        out_specs=VMEM,
        out_shape=jax.ShapeDtypeStruct((spread, 2, piece, rank), BF),
        compiler_params=PARAMS,
        name="add_up_through",
    )(got, bands)
    total = pl.pallas_call(
        hold,
        in_specs=[ANY, ANY],
        out_specs=ANY,
        out_shape=like(total),
        input_output_aliases={0: 0},
        compiler_params=PARAMS,
        name="hold",
    )(total, far)
    mats = exchange(total, SPREAD, list(range(spread))[::-1]).reshape(2, reducers, 2, piece, rank)

    return pl.pallas_call(
        finish,
        in_specs=[SMEM, VMEM, VMEM, VMEM, VMEM],
        out_specs=HBM,
        out_shape=jax.ShapeDtypeStruct((dims, rows, rank), BF),
        scratch_shapes=[pltpu.VMEM((2, STEPS, quarter, rank), BF), pltpu.SemaphoreType.DMA((2, STEPS))],
        compiler_params=PARAMS,
        name="finish",
    )(pos, mats, met, far, weights)


def solution(mesh):
    pts = mesh.shape["pts"]
    zh = pts // 16
    fine = Mesh(mesh.devices.reshape(2, zh, 2, 4, 2, 2), ("xl", "zh", "z1", "y", "xh", "core"))
    dim = ("xh", "core")
    points = ("xl", "zh", "z1", "y")
    return jax.shard_map(
        per_device,
        mesh=fine,
        in_specs=(P(dim, points, None), P(dim, None, None), P(points), P(None, points)),
        out_specs=P(dim, points, None),
        check_vma=False,
    )
```
